32 devices in a mesh: section: 4 (over x, core), seq: 8 (over z, y).
Axes of the slice: x: 2, y: 2, z: 4, core: 2. Of those that a mesh axis runs over, the one named last changes fastest.
Arguments:
- latents: bfloat16 [4, 256, 3072], P(None, 'seq'), may hold values from -6 to 6
- qkv_weight: bfloat16 [4, 3072, 16, 384], P('section', None, 'seq'), may hold values from -0.109375 to 0.109375
- out_weight: bfloat16 [4, 2048, 3072], P('section', 'seq'), may hold values from -0.125 to 0.125
- modulation: float32 [4, 3, 3072], P('section'), may hold values from -4 to 4
- qk_gain: float32 [4, 2, 128], P('section'), may hold values from 0.3 to 4
- stale_kv: bfloat16 [4, 1024, 16, 256], P('section', None, 'seq'), may hold values from -12 to 12
- patch_lengths: int32 [4], replicated, may hold values from 1 to 256, 768 in all
- refresh_at: int32 [4], replicated, may hold values from 1 to 4, as said below
Outputs:
- block_out: bfloat16 [4, 4, 256, 3072], P('section', None, 'seq')
- kv_next: bfloat16 [4, 1024, 16, 256], P('section', None, 'seq')
The draws below stay inside these ranges and needn't reach their ends.
Inputs may be any that keep to these rules, and one draw needn't show every extreme that they name: refresh_at[j] > j for every patch j; refresh_at[0] = 1; refresh_at[3] = 4.
All inputs are finite; a program needn't handle non-finite values.
Results may differ from the reference program's by a relative error of at most 0.038.
Values may be sent and summed in bfloat16 or wider, within the bound.
A program may use at most 64 MiB of HBM per device.

```python
import math
import jax
import jax.numpy as jnp
import numpy as np
from jax import lax

D = 3072
HEADS = 16
HD = 128
PATCHES = 4
PATCH_ROWS = 256
TOKENS = 1024
BLOCKS = 4
N_SECTION = 4
N_SEQ = 8


def draw_qk_gain(key, part):
    key = jax.random.fold_in(key, 11)
    raw = jax.random.uniform(key, (N_SECTION, 2, HD), jnp.float32, jnp.log(0.3), jnp.log(3.0))
    return jnp.exp(raw).astype(jnp.float32)


def draw_refresh_at(key, part):
    key = jax.random.fold_in(key, 23)
    ids = jnp.arange(PATCHES, dtype=jnp.int32)
    later = jax.random.randint(key, (PATCHES,), 0, PATCHES - ids, dtype=jnp.int32)
    later = jnp.where(ids == 0, 0, later).astype(jnp.int32)
    return jnp.minimum(ids + 1 + later, PATCHES).astype(jnp.int32)


def block_levels(key, shape, split, least, top_value):
    level, own = 1.0, jax.random.fold_in(key, 6)
    for position, blocks in split:
        steps = jnp.exp(jax.random.uniform(jax.random.fold_in(own, position), (blocks,), jnp.float32, least / len(split), top_value / len(split)))
        level = level * jnp.repeat(steps, shape[position] // blocks).reshape([-1 if axis == position else 1 for axis in range(len(shape))])
    return level


def length_profile(number_of, total, limit, lean):
    portions = [(1 << 20) // math.isqrt(grade ** lean) + 1 for grade in range(2, number_of + 1)]
    rest, holding = total - limit - (number_of - 1), [1] * (number_of - 1)
    while rest > 0:
        candidates = [i for i in range(number_of - 1) if holding[i] < limit]
        whole, remaining = sum([portions[i] for i in candidates]), rest
        for i in candidates:
            addition = min(limit - holding[i], max(1, remaining * portions[i] // whole), rest)
            holding[i] = holding[i] + addition
            rest = rest - addition
    return np.array([limit] + holding)


def ragged_sizes(stream_key, count, total, reach, skew):
    if count == 2:
        one = jax.random.randint(stream_key, (), max(1, total - reach), min(reach, total - 1) + 1)
        return jnp.stack([one, total - one])
    tallies = jnp.asarray(length_profile(count, total, reach, skew), jnp.int32)
    twos = (count - 1) // 2
    donor, sink = tallies[1:1 + 2 * twos:2], tallies[2:2 + 2 * twos:2]
    margin = jnp.minimum(donor - 1, reach - sink)
    passed = jax.random.randint(jax.random.fold_in(stream_key, 1), (twos,), 0, 1 << 20) % (margin + 1)
    tallies = tallies.at[1:1 + 2 * twos:2].set(donor - passed).at[2:2 + 2 * twos:2].set(sink + passed)
    return tallies[jax.random.permutation(jax.random.fold_in(stream_key, 2), count)]


def gaussian(stream_key, shape, scale, most, pieces=(), held_as=jnp.bfloat16):
    entries = jax.random.normal(stream_key, shape, jnp.float32) * scale
    if len(pieces) > 0:
        entries = block_levels(stream_key, shape, pieces, -0.22, 0.18) * entries
    return jnp.clip(entries, min=-most, max=most).astype(held_as)


def setup_inputs(seed: int = 0) -> dict:
    seeds = jax.random.split(jax.random.key(seed), 9)
    latents = gaussian(seeds[0], (PATCHES, PATCH_ROWS, D), 1.0, 6.0, ((1, 8),))
    qkv_weight = gaussian(seeds[1], (BLOCKS, D, HEADS, 3 * HD), D ** -0.5, 0.109375, ((0, 4), (2, 8)))
    out_weight = gaussian(seeds[2], (BLOCKS, HEADS * HD, D), (HEADS * HD) ** -0.5, 0.125, ((0, 4), (1, 8)))
    modulation = gaussian(seeds[3], (BLOCKS, 3, D), 1.0, 4.0, ((0, 4),), jnp.float32)
    qk_gain = draw_qk_gain(jax.random.fold_in(seeds[8], 71), 0)
    stale_kv = gaussian(seeds[5], (BLOCKS, TOKENS, HEADS, 2 * HD), 2.0, 12.0, ((0, 4), (2, 8)))
    patch_lengths = ragged_sizes(seeds[6], PATCHES, PATCHES * PATCH_ROWS * 3 // 4, PATCH_ROWS, 0).astype(jnp.int32)
    refresh_at = draw_refresh_at(jax.random.fold_in(seeds[8], 71), 0)
    return dict(latents=latents, qkv_weight=qkv_weight, out_weight=out_weight, modulation=modulation, qk_gain=qk_gain, stale_kv=stale_kv, patch_lengths=patch_lengths, refresh_at=refresh_at)


def run_block(rows, wqkv, wout, modvec, gains, stale, fresh, live, refresh_at, m, groups):
    patches, prow, heads, twice = stale.shape
    hd = twice // 2
    width = rows.shape[-1]
    x = rows.astype(jnp.float32)
    mean = lax.optimization_barrier(jnp.mean(x, axis=-1, keepdims=True))
    var = lax.optimization_barrier(jnp.mean((x - mean) ** 2, axis=-1, keepdims=True))
    normed = ((x - mean) * jax.lax.rsqrt(var + 1e-06) * (1.0 + modvec[1]) + modvec[0]).astype(jnp.bfloat16)
    qkv = jnp.dot(normed, wqkv.reshape(wqkv.shape[0], -1), preferred_element_type=jnp.float32)
    qkv = qkv.reshape(prow, heads, 3 * hd)
    query = qkv[..., :hd]
    key = qkv[..., hd:2 * hd]
    value = qkv[..., 2 * hd:]
    query = (query * jax.lax.rsqrt(lax.optimization_barrier(jnp.mean(query * query, axis=-1, keepdims=True)) + 1e-06) * gains[0]).astype(jnp.bfloat16)
    key = (key * jax.lax.rsqrt(lax.optimization_barrier(jnp.mean(key * key, axis=-1, keepdims=True)) + 1e-06) * gains[1]).astype(jnp.bfloat16)
    newkv = jnp.concatenate([key, value.astype(jnp.bfloat16)], axis=-1)
    fresh = fresh.at[m].set(newkv)
    ids = jnp.arange(patches)
    use_fresh = (ids == m) | (refresh_at <= m)
    keys_all = jnp.where(use_fresh[:, None, None, None], fresh, stale).reshape(patches * prow, heads, twice)
    keys = keys_all[..., :hd].astype(jnp.float32)
    values = keys_all[..., hd:].astype(jnp.float32)
    scores = jnp.einsum('qhd,khd->hqk', query.astype(jnp.float32), keys) / jnp.sqrt(jnp.float32(hd))
    scores = jnp.where(live[None, None, :], scores, jnp.float32(-1e+30))
    top = lax.optimization_barrier(jnp.max(scores, axis=-1, keepdims=True))
    expo = jnp.exp(scores - top)
    weights = (expo / lax.optimization_barrier(jnp.sum(expo, axis=-1, keepdims=True))).astype(jnp.bfloat16)
    attn = jnp.einsum('hqk,khd->qhd', weights.astype(jnp.float32), values).astype(jnp.bfloat16)
    attn_groups = attn.reshape(prow, groups, heads * hd // groups).astype(jnp.float32)
    out_groups = wout.reshape(groups, heads * hd // groups, width).astype(jnp.float32)
    partials = jnp.einsum('rgk,gkd->rgd', attn_groups, out_groups).astype(jnp.bfloat16)
    proj = lax.optimization_barrier(jnp.sum(partials.astype(jnp.float32), axis=1))
    return ((x + modvec[2] * proj).astype(jnp.bfloat16), fresh)

def reference(latents, qkv_weight, out_weight, modulation, qk_gain, stale_kv, patch_lengths, refresh_at):
    patches, prow, width = latents.shape
    heads = qkv_weight.shape[2]
    hd = qk_gain.shape[2]
    live = (jnp.arange(prow)[None, :] < patch_lengths[:, None]).reshape(-1)
    current = latents
    outs = []
    kvs = []
    for section in range(N_SECTION):
        stale = stale_kv[section].reshape(patches, prow, heads, 2 * hd)
        fresh = jnp.zeros_like(stale)
        produced = []
        for m in range(patches):
            rows, fresh = run_block(current[m], qkv_weight[section], out_weight[section], modulation[section], qk_gain[section], stale, fresh, live, refresh_at, m, N_SEQ)
            produced.append(rows)
        current = jnp.stack(produced)
        outs.append(current)
        kvs.append(fresh.reshape(patches * prow, heads, 2 * hd))
    return (jnp.stack(outs), jnp.stack(kvs))
```

```python
import functools

import jax
import jax.numpy as jnp
from jax import lax
from jax.experimental import pallas as pl
from jax.experimental.pallas import tpu as pltpu
from jax.sharding import PartitionSpec as P

MESH = pl.DeviceIdType.MESH


def kernel(
    dims,
    latents,
    w_qkv,
    w_out,
    modvec,
    gains,
    stale,
    lengths,
    refresh_at,
    block_out,
    kv_next,
    incoming,
    gathered,
    queries,
    kv_now,
    partial,
    col_in,
    line_out,
    line_in,
    gz_send,
    gy_send,
    g_recv,
    py_send,
    py_recv,
    pz_send,
    pz_recv,
    hop_send,
    hop_recv,
):
    sections, zs, ys, heads, hd = dims
    patches, rows, width = latents.shape
    patch_rows = zs * ys * rows
    col_rows = zs * rows
    sec = lax.axis_index("section")
    me = lax.axis_index("seq")
    z = lax.div(me, ys)
    y = lax.rem(me, ys)

    def dev(zz, yy):
        return (sec, zz * ys + yy)

    def zpart(zz):
        return pl.ds(pl.multiple_of(zz * rows, rows), rows)

    def remote(src, dst, send, recv, where):
        return pltpu.make_async_remote_copy(
            src_ref=src,
            dst_ref=dst,
            send_sem=send,
            recv_sem=recv,
            device_id=where,
            device_id_type=MESH,
        )

    barrier = pltpu.get_barrier_semaphore()
    for d in range(1, zs):
        pl.semaphore_signal(
            barrier, inc=1, device_id=dev(lax.rem(z + d, zs), y), device_id_type=MESH
        )
    for c in range(1, ys):
        pl.semaphore_signal(
            barrier, inc=1, device_id=dev(z, lax.rem(y + c, ys)), device_id_type=MESH
        )
    for step in (1, sections - 1):
        pl.semaphore_signal(
            barrier, inc=1, device_id=(lax.rem(sec + step, sections), me), device_id_type=MESH
        )
    pl.semaphore_wait(barrier, zs + ys)

    def hop(m):
        return remote(
            block_out.at[m], incoming.at[m], hop_send.at[m], hop_recv.at[m], (sec + 1, me)
        )

    def block_copy(yy, zz, send, where):
        spot = gathered.at[yy, zpart(zz), :]
        return remote(spot, spot, send, g_recv.at[yy, zz], where)

    def project(m, yy):
        qkv = jnp.dot(gathered[yy], w_qkv[...], preferred_element_type=jnp.float32)
        for h in range(heads):
            at = 3 * hd * h
            query = qkv[:, at : at + hd]
            key = qkv[:, at + hd : at + 2 * hd]
            value = qkv[:, at + 2 * hd : at + 3 * hd].astype(jnp.bfloat16)
            query = query * lax.rsqrt(jnp.mean(query * query, axis=-1, keepdims=True) + 1e-06)
            query = (query * gains[0:1, :]).astype(jnp.bfloat16)
            key = key * lax.rsqrt(jnp.mean(key * key, axis=-1, keepdims=True) + 1e-06)
            key = (key * gains[1:2, :]).astype(jnp.bfloat16)
            queries[yy, :, h * hd : (h + 1) * hd] = query
            for zz in range(zs):
                start = m * patch_rows + (zz * ys + yy) * rows
                spot = pl.ds(pl.multiple_of(start, rows), rows)
                piece = slice(zz * rows, (zz + 1) * rows)
                k_at = slice(2 * hd * h, 2 * hd * h + hd)
                v_at = slice(2 * hd * h + hd, 2 * hd * (h + 1))
                kv_next[spot, k_at] = key[piece]
                kv_next[spot, v_at] = value[piece]
                kv_now[spot, k_at] = key[piece]
                kv_now[spot, v_at] = value[piece]

    def attend(yy, slot):
        outs = []
        scale = hd**-0.5
        slots = lax.broadcasted_iota(jnp.int32, (1, patch_rows), 1)
        for h in range(heads):
            query = queries[yy, :, h * hd : (h + 1) * hd]
            key = kv_now[:, 2 * hd * h : 2 * hd * h + hd]
            value = kv_now[:, 2 * hd * h + hd : 2 * hd * (h + 1)]
            scores = lax.dot_general(
                query, key, (((1,), (1,)), ((), ())), preferred_element_type=jnp.float32
            )
            live = [
                jnp.where(
                    slots < lengths[j],
                    scores[:, j * patch_rows : (j + 1) * patch_rows],
                    jnp.float32(-1e30),
                )
                for j in range(patches)
            ]
            scores = jnp.concatenate(live, axis=1)
            top = jnp.max(scores, axis=-1, keepdims=True)
            expo = jnp.exp((scores - top) * scale)
            total = jnp.sum(expo, axis=-1, keepdims=True)
            attn = jnp.dot(expo.astype(jnp.bfloat16), value, preferred_element_type=jnp.float32)
            outs.append((attn / total).astype(jnp.bfloat16))
        attn = jnp.concatenate(outs, axis=1)
        partial[slot] = jnp.dot(attn, w_out[...], preferred_element_type=jnp.float32).astype(
            jnp.bfloat16
        )

    def patch_step(m, _):
        @pl.when(sec == 0)
        def _():
            incoming[m] = latents[m]

        @pl.when(sec > 0)
        def _():
            hop(m).wait_recv()

        x = incoming[m].astype(jnp.float32)
        mean = jnp.mean(x, axis=-1, keepdims=True)
        var = jnp.mean((x - mean) ** 2, axis=-1, keepdims=True)
        normed = (x - mean) * lax.rsqrt(var + 1e-06) * (1.0 + modvec[1:2, :]) + modvec[0:1, :]
        gathered[y, zpart(z), :] = normed.astype(jnp.bfloat16)

        sends = []
        for d in range(1, zs):
            sends.append(block_copy(y, z, gz_send.at[d - 1], dev(lax.rem(z + d, zs), y)))
            sends[-1].start()
        for d in range(zs):
            zz = lax.rem(z + zs - d, zs)
            if d > 0:
                block_copy(y, zz, gz_send.at[d - 1], dev(zz, y)).wait_recv()
            for c in range(1, ys):
                sends.append(
                    block_copy(y, zz, gy_send.at[c - 1, d], dev(z, lax.rem(y + c, ys)))
                )
                sends[-1].start()
            if d == 0:
                for j in range(patches):
                    part = slice(j * patch_rows, (j + 1) * patch_rows)
                    kv_now[part, :] = jnp.where(
                        refresh_at[j] <= m, kv_next[part, :], stale[part, :]
                    )
        project(m, y)
        for c in range(1, ys):
            yy = lax.rem(y + c, ys)
            for d in range(zs):
                zz = lax.rem(z + zs - d, zs)
                block_copy(yy, zz, gy_send.at[c - 1, d], dev(z, yy)).wait_recv()
            project(m, yy)
        for copy in sends:
            copy.wait_send()

        sends = []
        for c in range(1, ys):
            yy = lax.rem(y + c, ys)
            attend(yy, c)
            for k in list(range(1, zs)) + [0]:
                zz = lax.rem(z + k, zs)
                copy = remote(
                    partial.at[c, zpart(zz), :],
                    col_in.at[c - 1, k],
                    py_send.at[c - 1, k],
                    py_recv.at[c - 1, k],
                    dev(z, yy),
                )
                copy.start()
                sends.append(copy)
        attend(y, 0)

        def column_sum(k):
            total = partial[0, zpart(lax.rem(z + k, zs)), :].astype(jnp.float32)
            for c in range(1, ys):
                remote(
                    partial.at[c, zpart(z), :],
                    col_in.at[c - 1, k],
                    py_send.at[c - 1, k],
                    py_recv.at[c - 1, k],
                    dev(z, lax.rem(y + c, ys)),
                ).wait_recv()
                total = total + col_in[c - 1, k].astype(jnp.float32)
            return total

        def line(k):
            return remote(
                line_out.at[k - 1],
                line_in.at[k - 1],
                pz_send.at[k - 1],
                pz_recv.at[k - 1],
                dev(lax.rem(z + k, zs), y),
            )

        for k in range(1, zs):
            line_out[k - 1] = column_sum(k).astype(jnp.bfloat16)
            sends.append(line(k))
            sends[-1].start()
        proj = column_sum(0)
        for k in range(1, zs):
            line(k).wait_recv()
            proj = proj + line_in[k - 1].astype(jnp.float32)
        x = incoming[m].astype(jnp.float32)
        block_out[m] = (x + modvec[2:3, :] * proj).astype(jnp.bfloat16)

        @pl.when(sec < sections - 1)
        def _():
            hop(m).start()

        for copy in sends:
            copy.wait_send()
        return 0

    lax.fori_loop(0, patches, patch_step, 0)

    @pl.when(sec < sections - 1)
    def _():
        for m in range(patches):
            hop(m).wait_send()


def shards(
    mesh_shape,
    latents,
    qkv_weight,
    out_weight,
    modulation,
    qk_gain,
    stale_kv,
    patch_lengths,
    refresh_at,
):
    sections, seq = mesh_shape
    zs = min(4, seq)
    ys = seq // zs
    patches, rows, width = latents.shape
    heads = qkv_weight.shape[2]
    hd = qk_gain.shape[2]
    tokens = stale_kv.shape[1]
    bf16 = jnp.bfloat16
    vmem = pl.BlockSpec(memory_space=pltpu.VMEM)
    smem = pl.BlockSpec(memory_space=pltpu.SMEM)
    dma = pltpu.SemaphoreType.DMA
    others = max(ys - 1, 1)
    out, kv = pl.pallas_call(
        functools.partial(kernel, (sections, zs, ys, heads, hd)),
        out_shape=(
            jax.ShapeDtypeStruct((patches, rows, width), bf16),
            jax.ShapeDtypeStruct((tokens, heads * 2 * hd), bf16),
        ),
        in_specs=[vmem] * 6 + [smem] * 2,
        out_specs=(vmem, vmem),
        scratch_shapes=[
            pltpu.VMEM((patches, rows, width), bf16),
            pltpu.VMEM((ys, zs * rows, width), bf16),
            pltpu.VMEM((ys, zs * rows, heads * hd), bf16),
            pltpu.VMEM((tokens, heads * 2 * hd), bf16),
            pltpu.VMEM((ys, zs * rows, width), bf16),
            pltpu.VMEM((others, zs, rows, width), bf16),
            pltpu.VMEM((zs - 1, rows, width), bf16),
            pltpu.VMEM((zs - 1, rows, width), bf16),
            dma((zs - 1,)),
            dma((others, zs)),
            dma((ys, zs)),
            dma((others, zs)),
            dma((others, zs)),
            dma((zs - 1,)),
            dma((zs - 1,)),
            dma((patches,)),
            dma((patches,)),
        ],
        compiler_params=pltpu.CompilerParams(
            collective_id=0, has_side_effects=True, vmem_limit_bytes=56 * 1024 * 1024
        ),
    )(
        latents,
        qkv_weight[0].reshape(width, heads * 3 * hd),
        out_weight[0],
        modulation[0],
        qk_gain[0],
        stale_kv[0].reshape(tokens, heads * 2 * hd),
        patch_lengths,
        refresh_at,
    )
    return out[None], kv.reshape(1, tokens, heads, 2 * hd)


def solution(mesh):
    placed = (
        P(None, "seq", None),
        P("section", None, "seq", None),
        P("section", "seq", None),
        P("section", None, None),
        P("section", None, None),
        P("section", None, "seq", None),
        P(),
        P(),
    )
    return jax.shard_map(
        functools.partial(shards, (mesh.shape["section"], mesh.shape["seq"])),
        mesh=mesh,
        in_specs=placed,
        out_specs=(P("section", None, "seq", None), P("section", None, "seq", None)),
        check_vma=False,
    )
```

```python
import functools

import jax
import jax.numpy as jnp
from jax import lax
from jax.experimental import pallas as pl
from jax.experimental.pallas import tpu as pltpu
from jax.sharding import PartitionSpec as P

MESH = pl.DeviceIdType.MESH


def kernel(
    dims,
    latents,
    w_qkv,
    w_out,
    modvec,
    gains,
    stale,
    lengths,
    refresh_at,
    block_out,
    kv_next,
    incoming,
    gathered,
    queries,
    kv_now,
    w_peer,
    attn_out,
    attn_in,
    partial,
    line_out,
    line_in,
    gz_send,
    gy_send,
    g_recv,
    w_send,
    w_recv,
    a_send,
    a_recv,
    l_send,
    l_recv,
    hop_send,
    hop_recv,
    go,
):
    sections, zs, ys, heads, hd = dims
    patches, rows, width = latents.shape
    patch_rows = zs * ys * rows
    parts = 2 if rows % 32 == 0 else 1
    cut = rows // parts
    sec = lax.axis_index("section")
    me = lax.axis_index("seq")
    z = lax.div(me, ys)
    y = lax.rem(me, ys)

    def dev(zz, yy):
        return (sec, zz * ys + yy)

    def zpart(zz):
        return pl.ds(pl.multiple_of(zz * rows, rows), rows)

    def piece_of(zz, part):
        return pl.ds(pl.multiple_of(zz * rows + part * cut, cut), cut)

    def remote(src, dst, send, recv, where):
        return pltpu.make_async_remote_copy(
            src_ref=src,
            dst_ref=dst,
            send_sem=send,
            recv_sem=recv,
            device_id=where,
            device_id_type=MESH,
        )

    barrier = pltpu.get_barrier_semaphore()
    for d in range(1, zs):
        pl.semaphore_signal(
            barrier, inc=1, device_id=dev(lax.rem(z + d, zs), y), device_id_type=MESH
        )
    for c in range(1, ys):
        pl.semaphore_signal(
            barrier, inc=1, device_id=dev(z, lax.rem(y + c, ys)), device_id_type=MESH
        )
    for step in (1, sections - 1):
        pl.semaphore_signal(
            barrier, inc=1, device_id=(lax.rem(sec + step, sections), me), device_id_type=MESH
        )
    pl.semaphore_wait(barrier, zs + ys)

    def hop(m, part):
        span = pl.ds(part * cut, cut)
        return remote(
            block_out.at[m, span, :],
            incoming.at[m, span, :],
            hop_send.at[m, part],
            hop_recv.at[m, part],
            (sec + 1, me),
        )

    def block_copy(yy, zz, part, send, where):
        spot = gathered.at[yy, piece_of(zz, part), :]
        return remote(spot, spot, send, g_recv.at[yy, zz, part], where)

    def project(m, yy):
        qkv = jnp.dot(gathered[yy], w_qkv[...], preferred_element_type=jnp.float32)
        for h in range(heads):
            at = 3 * hd * h
            query = qkv[:, at : at + hd]
            key = qkv[:, at + hd : at + 2 * hd]
            value = qkv[:, at + 2 * hd : at + 3 * hd].astype(jnp.bfloat16)
            query = query * lax.rsqrt(jnp.mean(query * query, axis=-1, keepdims=True) + 1e-06)
            query = (query * gains[0:1, :]).astype(jnp.bfloat16)
            key = key * lax.rsqrt(jnp.mean(key * key, axis=-1, keepdims=True) + 1e-06)
            key = (key * gains[1:2, :]).astype(jnp.bfloat16)
            queries[yy, :, h * hd : (h + 1) * hd] = query
            for zz in range(zs):
                start = m * patch_rows + (zz * ys + yy) * rows
                spot = pl.ds(pl.multiple_of(start, rows), rows)
                piece = slice(zz * rows, (zz + 1) * rows)
                k_at = slice(2 * hd * h, 2 * hd * h + hd)
                v_at = slice(2 * hd * h + hd, 2 * hd * (h + 1))
                kv_next[spot, k_at] = key[piece]
                kv_next[spot, v_at] = value[piece]
                kv_now[spot, k_at] = key[piece]
                kv_now[spot, v_at] = value[piece]

    def attend(yy, slot):
        outs = []
        scale = hd**-0.5
        slots = lax.broadcasted_iota(jnp.int32, (1, patch_rows), 1)
        for h in range(heads):
            query = queries[yy, :, h * hd : (h + 1) * hd]
            key = kv_now[:, 2 * hd * h : 2 * hd * h + hd]
            value = kv_now[:, 2 * hd * h + hd : 2 * hd * (h + 1)]
            scores = lax.dot_general(
                query, key, (((1,), (1,)), ((), ())), preferred_element_type=jnp.float32
            )
            live = [
                jnp.where(
                    slots < lengths[j],
                    scores[:, j * patch_rows : (j + 1) * patch_rows],
                    jnp.float32(-1e30),
                )
                for j in range(patches)
            ]
            scores = jnp.concatenate(live, axis=1)
            top = jnp.max(scores, axis=-1, keepdims=True)
            expo = jnp.exp((scores - top) * scale)
            total = jnp.sum(expo, axis=-1, keepdims=True)
            attn = jnp.dot(expo.astype(jnp.bfloat16), value, preferred_element_type=jnp.float32)
            outs.append((attn / total).astype(jnp.bfloat16))
        attn_out[slot] = jnp.concatenate(outs, axis=1)

    def weights(c):
        return remote(
            w_out, w_peer.at[c - 1], w_send.at[c - 1], w_recv.at[c - 1], dev(z, lax.rem(y + c, ys))
        )

    ends = (zs - 1, 0)
    steps = (1, -1)

    def block_on(zz, part, side):
        return block_copy(y, zz, part, gz_send.at[side, zz, part], dev(z + steps[side], y))

    def block_across(zz, part, c):
        where = dev(z, lax.rem(y + c, ys))
        return block_copy(y, zz, part, gy_send.at[c - 1, zz, part], where)

    def sum_on(k, part):
        span = pl.ds(part * cut, cut)
        return remote(
            line_out.at[k - 1, span, :],
            line_in.at[k - 1, span, :],
            l_send.at[k - 1, part],
            l_recv.at[k - 1, part],
            dev(lax.rem(z + k, zs), y),
        )

    @pl.when(sec > 0)
    def _():
        pl.semaphore_wait(go, 1)

    for c in range(1, ys):
        weights(c).start()

    def patch_step(m, _):
        @pl.when(sec == 0)
        def _():
            incoming[m] = latents[m]

        def start_part(part):
            span = slice(part * cut, (part + 1) * cut)

            @pl.when(sec > 0)
            def _():
                hop(m, part).wait_recv()

            x = incoming[m, span, :].astype(jnp.float32)
            mean = jnp.mean(x, axis=-1, keepdims=True)
            var = jnp.mean((x - mean) ** 2, axis=-1, keepdims=True)
            normed = (x - mean) * lax.rsqrt(var + 1e-06) * (1.0 + modvec[1:2, :]) + modvec[0:1, :]
            gathered[y, piece_of(z, part), :] = normed.astype(jnp.bfloat16)
            for side in range(2):

                @pl.when(z != ends[side])
                def _():
                    block_on(z, part, side).start()

            for c in range(1, ys):
                block_across(z, part, c).start()

        def pass_on(d, part):
            for side in range(2):
                zz = z - steps[side] * d

                @pl.when((zz >= 0) & (zz < zs))
                def _():
                    block_on(zz, part, 1 - side).wait_recv()

                    @pl.when(z != ends[side])
                    def _():
                        block_on(zz, part, side).start()

                    for c in range(1, ys):
                        block_across(zz, part, c).start()

        start_part(0)
        for j in range(patches):
            part = slice(j * patch_rows, (j + 1) * patch_rows)
            kv_now[part, :] = jnp.where(refresh_at[j] <= m, kv_next[part, :], stale[part, :])
        for d in range(1, zs + parts - 1):
            for part in range(parts):
                if d - part == 0:
                    start_part(part)
                elif 0 < d - part < zs:
                    pass_on(d - part, part)

        project(m, y)
        for c in range(1, ys):
            yy = lax.rem(y + c, ys)
            for zz in range(zs):
                for part in range(parts):
                    send = gy_send.at[c - 1, zz, part]
                    block_copy(yy, zz, part, send, dev(z, yy)).wait_recv()
            project(m, yy)
        for d in range(zs):
            for side in range(2):
                zz = z - steps[side] * d

                @pl.when((zz >= 0) & (zz < zs) & (z != ends[side]))
                def _():
                    for part in range(parts):
                        block_on(zz, part, side).wait_send()

        for c in range(1, ys):
            for zz in range(zs):
                for part in range(parts):
                    block_across(zz, part, c).wait_send()

        def attn_copy(c):
            return remote(
                attn_out.at[c],
                attn_in.at[c - 1],
                a_send.at[c - 1],
                a_recv.at[c - 1],
                dev(z, lax.rem(y + c, ys)),
            )

        for c in range(1, ys):
            attend(lax.rem(y + c, ys), c)
            attn_copy(c).start()
        attend(y, 0)

        @pl.when(m == 0)
        def _():
            for c in range(1, ys):
                weights(c).wait_recv()

            @pl.when(sec < sections - 1)
            def _():
                pl.semaphore_signal(go, inc=1, device_id=(sec + 1, me), device_id_type=MESH)

        total = jnp.dot(attn_out[0], w_out[...], preferred_element_type=jnp.float32)
        for c in range(1, ys):
            attn_copy(c).wait_recv()
            total = total + jnp.dot(
                attn_in[c - 1], w_peer[c - 1], preferred_element_type=jnp.float32
            )
        partial[...] = total

        for part in range(parts):
            for k in range(1, zs):
                zz = lax.rem(z + k, zs)
                span = slice(part * cut, (part + 1) * cut)
                line_out[k - 1, span, :] = partial[piece_of(zz, part), :].astype(jnp.bfloat16)
                sum_on(k, part).start()

        for part in range(parts):
            span = slice(part * cut, (part + 1) * cut)
            proj = partial[piece_of(z, part), :]
            for k in range(1, zs):
                sum_on(k, part).wait_recv()
                proj = proj + line_in[k - 1, span, :].astype(jnp.float32)
            x = incoming[m, span, :].astype(jnp.float32)
            block_out[m, span, :] = (x + modvec[2:3, :] * proj).astype(jnp.bfloat16)

            @pl.when(sec < sections - 1)
            def _():
                hop(m, part).start()

        for c in range(1, ys):
            attn_copy(c).wait_send()
        for k in range(1, zs):
            for part in range(parts):
                sum_on(k, part).wait_send()

        return 0

    lax.fori_loop(0, patches, patch_step, 0)
    for c in range(1, ys):
        weights(c).wait_send()

    @pl.when(sec < sections - 1)
    def _():
        for m in range(patches):
            for part in range(parts):
                hop(m, part).wait_send()


def shards(
    mesh_shape,
    latents,
    qkv_weight,
    out_weight,
    modulation,
    qk_gain,
    stale_kv,
    patch_lengths,
    refresh_at,
):
    sections, seq = mesh_shape
    zs = min(4, seq)
    ys = seq // zs
    patches, rows, width = latents.shape
    heads = qkv_weight.shape[2]
    hd = qk_gain.shape[2]
    tokens = stale_kv.shape[1]
    bf16 = jnp.bfloat16
    vmem = pl.BlockSpec(memory_space=pltpu.VMEM)
    smem = pl.BlockSpec(memory_space=pltpu.SMEM)
    dma = pltpu.SemaphoreType.DMA
    others = max(ys - 1, 1)
    out, kv = pl.pallas_call(
        functools.partial(kernel, (sections, zs, ys, heads, hd)),
        out_shape=(
            jax.ShapeDtypeStruct((patches, rows, width), bf16),
            jax.ShapeDtypeStruct((tokens, heads * 2 * hd), bf16),
        ),
        in_specs=[vmem] * 6 + [smem] * 2,
        out_specs=(vmem, vmem),
        scratch_shapes=[
            pltpu.VMEM((patches, rows, width), bf16),
            pltpu.VMEM((ys, zs * rows, width), bf16),
            pltpu.VMEM((ys, zs * rows, heads * hd), bf16),
            pltpu.VMEM((tokens, heads * 2 * hd), bf16),
            pltpu.VMEM((others, heads * hd, width), bf16),
            pltpu.VMEM((ys, zs * rows, heads * hd), bf16),
            pltpu.VMEM((others, zs * rows, heads * hd), bf16),
            pltpu.VMEM((zs * rows, width), jnp.float32),
            pltpu.VMEM((zs - 1, rows, width), bf16),
            pltpu.VMEM((zs - 1, rows, width), bf16),
            dma((2, zs, 2)),
            dma((others, zs, 2)),
            dma((ys, zs, 2)),
            dma((others,)),
            dma((others,)),
            dma((others,)),
            dma((others,)),
            dma((zs - 1, 2)),
            dma((zs - 1, 2)),
            dma((patches, 2)),
            dma((patches, 2)),
            pltpu.SemaphoreType.REGULAR,
        ],
        compiler_params=pltpu.CompilerParams(
            collective_id=0, has_side_effects=True, vmem_limit_bytes=56 * 1024 * 1024
        ),
    )(
        latents,
        qkv_weight[0].reshape(width, heads * 3 * hd),
        out_weight[0],
        modulation[0],
        qk_gain[0],
        stale_kv[0].reshape(tokens, heads * 2 * hd),
        patch_lengths,
        refresh_at,
    )
    return out[None], kv.reshape(1, tokens, heads, 2 * hd)


def solution(mesh):
    placed = (
        P(None, "seq", None),
        P("section", None, "seq", None),
        P("section", "seq", None),
        P("section", None, None),
        P("section", None, None),
        P("section", None, "seq", None),
        P(),
        P(),
    )
    return jax.shard_map(
        functools.partial(shards, (mesh.shape["section"], mesh.shape["seq"])),
        mesh=mesh,
        in_specs=placed,
        out_specs=(P("section", None, "seq", None), P("section", None, "seq", None)),
        check_vma=False,
    )
```
